32 devices in a mesh: tok: 8 (over z, x), hid: 4 (over y, core).
Axes of the slice: x: 2, y: 2, z: 4, core: 2. Of those that a mesh axis runs over, the one named last changes fastest.
Arguments:
- tokens: bfloat16 [4096, 5376], P('tok', 'hid'), may hold values from -6 to 6
- norm_gain: bfloat16 [1, 5376], P(None, 'hid'), may hold values from 0.099609375 to 1.8984375
- w_query: bfloat16 [5376, 4096], P('tok', 'hid'), may hold values from -2 to 2
- w_key: bfloat16 [5376, 2048], P('tok', 'hid'), may hold values from -1 to 1
- value_matrix: bfloat16 [5376, 2048], P('tok', 'hid'), may hold values from -0.078125 to 0.078125
- q_norm_gain: bfloat16 [1, 128], replicated, may hold values from 0.1 to 8
- k_norm_gain: bfloat16 [1, 128], replicated, may hold values from 0.1 to 8
- w_out: bfloat16 [4096, 5376], P('hid'), may hold values from -0.125 to 0.125
Outputs:
- attended: bfloat16 [4096, 5376], P('tok', 'hid')
The draws below stay inside these ranges and needn't reach their ends.
All inputs are finite; a program needn't handle non-finite values.
Results may differ from the reference program's by a relative error of at most 0.017.
Values may be sent and summed in bfloat16 or wider, within the bound.
A program may use at most 128 MiB of HBM per device.

```python
import math
import jax
import jax.numpy as jnp
from jax import lax

MODEL_WIDTH = 5376
QUERY_HEADS = 32
KEY_VALUE_HEADS = 16
HEAD_SIZE = 128
WINDOW = 1024
TOKENS_PER_PART = 512
TOKENS = 4096
REACH = 2
N_HID = 4


def draw_pair(key):
    key_matrix = jax.random.truncated_normal(jax.random.fold_in(key, 101), -4.0, 4.0, (MODEL_WIDTH, KEY_VALUE_HEADS * HEAD_SIZE), jnp.float32) / math.sqrt(MODEL_WIDTH)
    query_weight = jax.random.truncated_normal(jax.random.fold_in(key, 102), -4.0, 4.0, (MODEL_WIDTH, QUERY_HEADS * HEAD_SIZE), jnp.float32) / math.sqrt(MODEL_WIDTH)
    return (query_weight, key_matrix)


def draw_w_query(key, part):
    return draw_pair(key)[0].astype(jnp.bfloat16)


def draw_w_key(key, part):
    return draw_pair(key)[1].astype(jnp.bfloat16)


def draw_head_gain(key, salt):
    inner = jax.random.fold_in(key, salt)
    gain = 1.0 + 0.18 * jax.random.truncated_normal(inner, -4.5, 4.5, (1, HEAD_SIZE), jnp.float32)
    return gain.astype(jnp.bfloat16)


def draw_q_norm_gain(key, part):
    return draw_head_gain(key, 201)


def draw_k_norm_gain(key, part):
    return draw_head_gain(key, 202)


def with_spikes(drawn, key, source, target, blocks, factor):
    owner, partner = [(jnp.arange(drawn.shape[dim]) // (drawn.shape[dim] // blocks)).reshape([-1 if axis == dim else 1 for axis in range(drawn.ndim)]) for dim in (source, target)]
    chosen = jax.random.permutation(key, blocks)[partner]
    strong = (owner == chosen) | (owner == (partner + blocks // 2) % blocks)
    return jnp.where(strong, factor * drawn, drawn)


def steps_of(key, extent, pieces, least, largest):
    loudness = 1.0
    for axis_at, shards_of in pieces:
        draws = jax.random.uniform(jax.random.fold_in(jax.random.fold_in(key, 6), axis_at), (shards_of,), jnp.float32, least / len(pieces), largest / len(pieces))
        loudness = loudness * jnp.repeat(jnp.exp(draws), extent[axis_at] // shards_of).reshape((-1,) + (1,) * (len(extent) - 1 - axis_at))
    return loudness


def noise(own_key, dims, spread, limit, split=(), kind=jnp.bfloat16):
    array = spread * jax.random.normal(own_key, dims, jnp.float32)
    if split:
        array = array * steps_of(own_key, dims, split, -0.22, 0.18)
    return jnp.clip(array, -limit, limit).astype(kind)


def heavy_noise(own_key, extent, deviation, reach, pieces, heavy, kind=jnp.bfloat16):
    result = deviation * jax.random.normal(own_key, extent, jnp.float32)
    if pieces:
        result = result * steps_of(own_key, extent, pieces, -0.22, 0.18)
    return jnp.clip(with_spikes(result, jax.random.fold_in(own_key, 3), *heavy), -reach, reach).astype(kind)


def setup_inputs(seed: int = 0) -> dict:
    seeds = jax.random.split(jax.random.key(seed), 9)
    return {
        "tokens": noise(seeds[0], (TOKENS, MODEL_WIDTH), 1.0, 6.0, ((0, 8), (1, 4))),
        "norm_gain": jnp.clip(1.0 + 0.18 * jax.random.normal(seeds[1], (1, MODEL_WIDTH), jnp.float32), 0.099609375, 1.8984375).astype(jnp.bfloat16),
        "w_query": draw_w_query(jax.random.fold_in(seeds[8], 71), 0),
        "w_key": draw_w_key(jax.random.fold_in(seeds[8], 71), 0),
        "value_matrix": noise(seeds[4], (MODEL_WIDTH, KEY_VALUE_HEADS * HEAD_SIZE), MODEL_WIDTH ** -0.5, 0.078125, ((0, 8), (1, 4))),
        "q_norm_gain": draw_q_norm_gain(jax.random.fold_in(seeds[8], 71), 0),
        "k_norm_gain": draw_k_norm_gain(jax.random.fold_in(seeds[8], 71), 0),
        "w_out": heavy_noise(seeds[7], (QUERY_HEADS * HEAD_SIZE, MODEL_WIDTH), (QUERY_HEADS * HEAD_SIZE) ** -0.5, 0.125, ((0, 4),), (0, 1, 4, 2.0)),
    }


score_scale = 168.0 ** (-0.5)

def head_norm(field, gain):
    count = field.shape[0]
    heads = field.reshape(count, -1, HEAD_SIZE)
    mean_square = lax.optimization_barrier(jnp.mean(heads * heads, axis=-1, keepdims=True))
    scaled = heads * lax.rsqrt(mean_square + 1e-06) * gain.astype(jnp.float32).reshape(1, 1, HEAD_SIZE)
    return scaled.reshape(count, -1)

def rotate(field, positions):
    count = field.shape[0]
    heads = field.reshape(count, -1, HEAD_SIZE)
    half = HEAD_SIZE // 2
    inverse = jnp.exp(-math.log(10000.0) * jnp.arange(half, dtype=jnp.float32) * 2.0 / HEAD_SIZE)
    angles = positions.astype(jnp.float32)[:, None] * inverse[None, :]
    cosine = jnp.cos(angles)[:, None, :]
    sine = jnp.sin(angles)[:, None, :]
    first = heads[..., :half]
    second = heads[..., half:]
    turned = jnp.concatenate([first * cosine - second * sine, second * cosine + first * sine], axis=-1)
    return turned.reshape(count, -1)

def reference(tokens, norm_gain, w_query, w_key, value_matrix, q_norm_gain, k_norm_gain, w_out):
    values32 = tokens.astype(jnp.float32)
    scale_rows = lax.rsqrt(lax.optimization_barrier(jnp.mean(values32 * values32, axis=1, keepdims=True)) + 1e-06)
    normed = (values32 * scale_rows * norm_gain.astype(jnp.float32)).astype(jnp.bfloat16)
    positions = jnp.arange(TOKENS, dtype=jnp.int32)
    query_raw = jnp.dot(normed, w_query, preferred_element_type=jnp.float32)
    key_raw = jnp.dot(normed, w_key, preferred_element_type=jnp.float32)
    query = rotate(head_norm(query_raw, q_norm_gain), positions).astype(jnp.bfloat16)
    key = rotate(head_norm(key_raw, k_norm_gain), positions).astype(jnp.bfloat16)
    value_rows = jnp.dot(normed, value_matrix, preferred_element_type=jnp.float32).astype(jnp.bfloat16)
    leading_part = REACH * TOKENS_PER_PART
    padded_keys = jnp.concatenate([jnp.zeros((leading_part, KEY_VALUE_HEADS * HEAD_SIZE), jnp.bfloat16), key], axis=0)
    padded_values = jnp.concatenate([jnp.zeros((leading_part, KEY_VALUE_HEADS * HEAD_SIZE), jnp.bfloat16), value_rows], axis=0)
    query_group_count = QUERY_HEADS // KEY_VALUE_HEADS
    window_extent = (REACH + 1) * TOKENS_PER_PART

    def one_block(block):
        start = (block * TOKENS_PER_PART).astype(jnp.int32)
        query_tile_rows = lax.dynamic_slice_in_dim(query, start, TOKENS_PER_PART, 0)
        nearby_keys = lax.dynamic_slice_in_dim(padded_keys, start, window_extent, 0)
        nearby_values = lax.dynamic_slice_in_dim(padded_values, start, window_extent, 0)
        query_pos = start + jnp.arange(TOKENS_PER_PART, dtype=jnp.int32)
        key_pos = start - leading_part + jnp.arange(window_extent, dtype=jnp.int32)
        query_four_axes = query_tile_rows.reshape(TOKENS_PER_PART, KEY_VALUE_HEADS, query_group_count, HEAD_SIZE).astype(jnp.float32)
        keys_three_axes = nearby_keys.reshape(window_extent, KEY_VALUE_HEADS, HEAD_SIZE).astype(jnp.float32)
        values_three_axes = nearby_values.reshape(window_extent, KEY_VALUE_HEADS, HEAD_SIZE).astype(jnp.float32)
        scores = jnp.einsum('tkgd,skd->kgts', query_four_axes, keys_three_axes) * score_scale
        allowed = (key_pos[None, :] <= query_pos[:, None]) & (key_pos[None, :] > query_pos[:, None] - WINDOW) & (key_pos[None, :] >= 0)
        masked = jnp.where(allowed, scores, -1e+30)
        top = lax.optimization_barrier(jnp.max(masked, axis=-1, keepdims=True))
        weights = jnp.where(allowed, jnp.exp(masked - top), 0.0)
        total = lax.optimization_barrier(jnp.sum(weights, axis=-1))
        probs = weights.astype(jnp.bfloat16).astype(jnp.float32)
        mixed = jnp.einsum('kgts,skd->tkgd', probs, values_three_axes)
        mixed = mixed / jnp.transpose(total, (2, 0, 1))[..., None]
        return mixed.reshape(TOKENS_PER_PART, QUERY_HEADS * HEAD_SIZE).astype(jnp.bfloat16)
    blocks = lax.map(one_block, jnp.arange(TOKENS // TOKENS_PER_PART, dtype=jnp.int32))
    heads_out = blocks.reshape(TOKENS, QUERY_HEADS * HEAD_SIZE)
    block_width = QUERY_HEADS * HEAD_SIZE // N_HID
    summed = jnp.zeros((TOKENS, MODEL_WIDTH), jnp.float32)
    for block in range(N_HID):
        part = jnp.dot(heads_out[:, block * block_width:(block + 1) * block_width], w_out[block * block_width:(block + 1) * block_width], preferred_element_type=jnp.float32)
        rounded = lax.optimization_barrier(part.astype(jnp.bfloat16))
        summed = summed + rounded.astype(jnp.float32)
    return summed.astype(jnp.bfloat16)
```

```python
import functools
import math

import jax
import jax.numpy as jnp
from jax import lax
from jax.experimental import pallas as pl
from jax.experimental.pallas import tpu as pltpu
from jax.sharding import PartitionSpec as P

HEAD = 128
WINDOW = 1024
SCALE = 168.0 ** (-0.5)
GAIN_ROWS = 16
MESH = pl.DeviceIdType.MESH
F32 = jnp.float32
BF16 = jnp.bfloat16


def tok_of(pos, n):
    pos = lax.rem(pos + 2 * n, n)
    return jnp.where(pos < n // 2, 2 * pos, 2 * (n - 1 - pos) + 1)


def project(n, nh, reach, x_ref, wq, wk, wv, qg, kg, cos_ref, sin_ref, q_out, win_out,
            w, xs, normed, acc, win, own_sem, x_send, x_recv, send_sem, recv_sem,
            halo_send, halo_recv):
    t = lax.axis_index("tok")
    h = lax.axis_index("hid")
    half = n // 2
    rows = q_out.shape[1]
    sub = x_ref.shape[0]
    part_heads = w.shape[3] // HEAD
    pos = jnp.where(lax.rem(t, 2) == 0, t // 2, n - 1 - t // 2)
    nxt = (tok_of(pos + 1, n), tok_of(pos - 1, n))

    barrier = pltpu.get_barrier_semaphore()
    near = list(nxt) + [lax.rem(t + d + n, n) for d in (1, -1, 2, -2)]
    for peer in near:
        pl.semaphore_signal(barrier, inc=1, device_id={"tok": peer}, device_id_type=MESH)
    for d in range(1, nh):
        pl.semaphore_signal(
            barrier, inc=1, device_id={"hid": lax.rem(h + d, nh)}, device_id_type=MESH)

    cols = w.shape[3]
    own = [
        pltpu.make_async_copy(src, w.at[t, p], own_sem.at[p])
        for p, src in enumerate((wk, wv, wq.at[:, pl.ds(0, cols)], wq.at[:, pl.ds(cols, cols)]))
    ]
    for copy in own:
        copy.start()
    own_x = pltpu.make_async_copy(x_ref, xs.at[h], own_sem.at[4])
    own_x.start()
    pl.semaphore_wait(barrier, len(near) + nh - 1)

    def hop(way, step, part):
        origin = tok_of(pos - step if way == 0 else pos + step, n)
        return pltpu.make_async_remote_copy(
            src_ref=w.at[origin, part], dst_ref=w.at[origin, part],
            send_sem=send_sem.at[way, step, part], recv_sem=recv_sem.at[way, step, part],
            device_id={"tok": nxt[way]}, device_id_type=MESH)

    def arrival(way, step, part):
        origin = tok_of(pos - step - 1 if way == 0 else pos + step + 1, n)
        return pltpu.make_async_remote_copy(
            src_ref=w.at[origin, part], dst_ref=w.at[origin, part],
            send_sem=send_sem.at[way, step, part], recv_sem=recv_sem.at[way, step, part],
            device_id={"tok": nxt[way]}, device_id_type=MESH)

    def carried(way, step, part):
        return step < half - 1 or part % 2 == way

    def launch(step, parts):
        for part in parts:
            for way in (0, 1):
                if carried(way, step, part):
                    if step == 0:
                        if way == 0:
                            own[part].wait()
                    else:
                        arrival(way, step - 1, part).wait_recv()
                    hop(way, step, part).start()

    def x_copy(d, slot):
        return pltpu.make_async_remote_copy(
            src_ref=x_ref, dst_ref=xs.at[slot], send_sem=x_send.at[d - 1],
            recv_sem=x_recv.at[d - 1],
            device_id={"hid": lax.rem(h + d, nh)}, device_id_type=MESH)

    kv, qq = (0, 1), (2, 3)
    launch(0, kv)
    for d in range(1, nh):
        x_copy(d, h).start()
    for step in range(1, half):
        launch(step, kv)
    launch(0, qq)

    own_x.wait()
    for d in range(1, nh):
        x_copy(d, lax.rem(h - d + nh, nh)).wait_recv()
    block = 128

    def norm_rows(i, _):
        at = pl.ds(pl.multiple_of(i * block, block), block)
        square = jnp.zeros((block, 1), F32)
        for b in range(nh):
            for j in range(sub):
                value = xs[b, j, at, :].astype(F32)
                square = square + jnp.sum(value * value, axis=1, keepdims=True)
        scale = lax.rsqrt(square / (nh * sub * x_ref.shape[2]) + 1e-06)
        for b in range(nh):
            for j in range(sub):
                value = xs[b, j, at, :].astype(F32)
                gain = xs[b, j, pl.ds(rows, GAIN_ROWS), :].astype(F32)[0:1]
                normed[b * sub + j, at, :] = (value * scale * gain).astype(BF16)
        return 0

    lax.fori_loop(0, rows // block, norm_rows, 0)

    def accumulate(part, slab):
        acc[part] += jnp.dot(normed[slab], w[slab, part], preferred_element_type=F32)

    def head_turned(part, j, gain):
        def place(i, _):
            at = pl.ds(pl.multiple_of(i * block, block), block)
            value = acc[part, at, j * HEAD:(j + 1) * HEAD]
            mean = jnp.sum(value * value, axis=1, keepdims=True) / HEAD
            value = value * lax.rsqrt(mean + 1e-06) * gain
            turned = value * cos_ref[at, :] + pltpu.roll(value, HEAD // 2, 1) * sin_ref[at, :]
            yield_at = turned.astype(BF16)
            if part == 0:
                at2 = pl.ds(pl.multiple_of(reach * rows + i * block, block), block)
                win[j, at2, :] = yield_at
            else:
                q_out[(part - 2) * part_heads + j, at, :] = yield_at
            return 0

        lax.fori_loop(0, rows // block, place, 0)

    for part in range(4):
        acc[part] = jnp.zeros(acc.shape[1:], F32)
    for way in (0, 1):
        arrival(way, half - 2, 1 - way).wait_recv()
        arrival(way, half - 1, way).wait_recv()

    def kv_slab(i, _):
        accumulate(0, i)
        accumulate(1, i)
        return 0

    lax.fori_loop(0, n, kv_slab, 0)
    k_gain = kg[...].astype(F32)
    q_gain = qg[...].astype(F32)
    for j in range(part_heads):
        head_turned(0, j, k_gain)
        win[part_heads + j, pl.ds(reach * rows, rows), :] = (
            acc[1, :, j * HEAD:(j + 1) * HEAD].astype(BF16))

    even = lax.rem(t, 2) == 0
    mine = win.at[:, pl.ds(2 * rows, rows), :]
    far = win.at[:, pl.ds(0, rows), :]
    mid = win.at[:, pl.ds(rows, rows), :]

    def halo(k, src, dst, peer):
        return pltpu.make_async_remote_copy(
            src_ref=src, dst_ref=dst, send_sem=halo_send.at[k], recv_sem=halo_recv.at[k],
            device_id={"tok": lax.rem(peer + n, n)}, device_id_type=MESH)

    to_far = halo(0, mine, far, t + 2)
    to_mid = halo(1, mine, mid, t + 1)
    relay = halo(1, far, mid, t - 1)
    has_far = t >= 2
    has_mid = t >= 1
    gives_far = t + 2 < n
    relays = jnp.logical_and(jnp.logical_not(even), has_far)

    @pl.when(gives_far)
    def _():
        to_far.start()

    @pl.when(even)
    def _():
        to_mid.start()

    @pl.when(jnp.logical_not(has_far))
    def _():
        win[:, pl.ds(0, rows), :] = jnp.zeros((win.shape[0], rows, HEAD), BF16)

    @pl.when(jnp.logical_not(has_mid))
    def _():
        win[:, pl.ds(rows, rows), :] = jnp.zeros((win.shape[0], rows, HEAD), BF16)

    for step in range(1, half):
        if step == half - 1:
            @pl.when(has_far)
            def _():
                to_far.wait_recv()

            @pl.when(relays)
            def _():
                relay.start()
        launch(step, qq)

    for way in (0, 1):
        arrival(way, half - 2, 3 - way).wait_recv()

    def q_slab(i, _):
        slab = tok_of(pos - (half - 1) + i, n)
        accumulate(2, slab)
        accumulate(3, slab)
        return 0

    lax.fori_loop(0, n - 1, q_slab, 0)
    last = tok_of(pos + half, n)
    for way in (0, 1):
        arrival(way, half - 1, 2 + way).wait_recv()
        accumulate(2 + way, last)
        for j in range(part_heads):
            head_turned(2 + way, j, q_gain)

    @pl.when(has_mid)
    def _():
        to_mid.wait_recv()

    win_out[...] = win[...]

    @pl.when(gives_far)
    def _():
        to_far.wait_send()

    @pl.when(even)
    def _():
        to_mid.wait_send()

    @pl.when(relays)
    def _():
        relay.wait_send()

    for d in range(1, nh):
        x_copy(d, h).wait_send()
    for parts in (kv, qq):
        for step in range(half):
            for part in parts:
                for way in (0, 1):
                    if carried(way, step, part):
                        hop(way, step, part).wait_send()


def attend(nh, reach, q_ref, win_ref, wo_ref, out_ref, heads, part, sib, pair, got,
           sib_send, sib_recv, y_send, y_recv):
    t = lax.axis_index("tok")
    h = lax.axis_index("hid")
    ny = nh // 2
    y, core = h // 2, lax.rem(h, 2)
    q_heads, rows = q_ref.shape[0], q_ref.shape[1]
    kv_heads = win_ref.shape[0] // 2
    group = q_heads // kv_heads
    width = out_ref.shape[1]
    block = rows // 2
    extent = block + WINDOW

    barrier = pltpu.get_barrier_semaphore()
    for d in range(1, nh):
        pl.semaphore_signal(
            barrier, inc=1, device_id={"hid": lax.rem(h + d, nh)}, device_id_type=MESH)

    def attention(r):
        ahead = reach * rows + r * block - WINDOW
        row = lax.broadcasted_iota(jnp.int32, (block, extent), 0)
        col = lax.broadcasted_iota(jnp.int32, (block, extent), 1)
        first = reach * rows - t * rows - ahead
        allowed = (col <= row + WINDOW) & (col > row) & (col >= first)

        def head(i, _):
            k = win_ref[i, pl.ds(ahead, extent), :]
            v = win_ref[kv_heads + i, pl.ds(ahead, extent), :]
            for g in range(group):
                q = q_ref[i * group + g, pl.ds(r * block, block), :]
                s = lax.dot_general(
                    q, k, (((1,), (1,)), ((), ())), preferred_element_type=F32) * SCALE
                s = jnp.where(allowed, s, -1e30)
                top = jnp.max(s, axis=1, keepdims=True)
                weights = jnp.exp(s - top)
                total = jnp.sum(weights, axis=1, keepdims=True)
                mixed = jnp.dot(weights.astype(BF16), v, preferred_element_type=F32) / total
                heads[i * group + g] = mixed.astype(BF16)
            return 0

        lax.fori_loop(0, kv_heads, head, 0)

    def to_sibling(r, k):
        y2 = lax.rem(y + k, ny)
        return pltpu.make_async_remote_copy(
            src_ref=part.at[r, y2 * 2 + 1 - core], dst_ref=sib.at[r, k],
            send_sem=sib_send.at[r, k], recv_sem=sib_recv.at[r, k],
            device_id={"hid": y * 2 + 1 - core}, device_id_type=MESH)

    def across(r, k):
        y2 = lax.rem(y + k, ny)
        return pltpu.make_async_remote_copy(
            src_ref=pair.at[r, k - 1], dst_ref=got.at[r, k - 1],
            send_sem=y_send.at[r, k - 1], recv_sem=y_recv.at[r, k - 1],
            device_id={"hid": y2 * 2 + core}, device_id_type=MESH)

    def out_project(r):
        mixed = jnp.concatenate([heads[i] for i in range(q_heads)], axis=1)
        for b in range(nh):
            start, end = b * width, (b + 1) * width
            a, e = start // 128 * 128, -(-end // 128) * 128
            value = jnp.dot(mixed, wo_ref[:, a:e], preferred_element_type=F32)
            if start > a:
                value = pltpu.roll(value, (e - a) - (start - a), 1)
            part[r, b] = value[:, :width].astype(BF16)

    order = list(range(1, ny)) + [0]

    def pass_on(r):
        for k in range(1, ny):
            to_sibling(r, k).wait_recv()
            y2 = lax.rem(y + k, ny)
            pair[r, k - 1] = (
                part[r, y2 * 2 + core].astype(F32) + sib[r, k].astype(F32)).astype(BF16)
            across(r, k).start()

    def finish(r):
        to_sibling(r, 0).wait_recv()
        value = part[r, h].astype(F32) + sib[r, 0].astype(F32)
        for k in range(1, ny):
            across(r, k).wait_recv()
            value = value + got[r, k - 1].astype(F32)
        out_ref[pl.ds(r * block, block), :] = value.astype(BF16)

    for r in range(2):
        attention(r)
        out_project(r)
        if r == 0:
            pl.semaphore_wait(barrier, nh - 1)
        for k in order:
            to_sibling(r, k).start()
        pass_on(r)
    for r in range(2):
        finish(r)
    for r in range(2):
        for k in order:
            to_sibling(r, k).wait_send()
        for k in range(1, ny):
            across(r, k).wait_send()


def local(n, nh, tokens, norm_gain, w_query, w_key, value_matrix, q_norm_gain, k_norm_gain, w_out):
    rows, feat = tokens.shape
    slab, kv_cols = w_key.shape
    sub = feat // slab
    q_heads, kv_heads = w_query.shape[1] // HEAD, kv_cols // HEAD
    reach = (WINDOW - 1 + rows - 1) // rows
    width = w_out.shape[1] // nh
    half = n // 2
    extended = jnp.concatenate(
        [tokens, jnp.broadcast_to(norm_gain, (GAIN_ROWS, feat))], axis=0)
    extended = jnp.transpose(extended.reshape(rows + GAIN_ROWS, sub, slab), (1, 0, 2))
    inverse = jnp.exp(
        -math.log(10000.0) * jnp.arange(HEAD // 2, dtype=F32) * 2.0 / HEAD)
    positions = lax.axis_index("tok") * rows + jnp.arange(rows, dtype=jnp.int32)
    angles = positions.astype(F32)[:, None] * inverse[None, :]
    cosine, sine = jnp.cos(angles), jnp.sin(angles)
    cosine = jnp.concatenate([cosine, cosine], axis=1)
    sine = jnp.concatenate([-sine, sine], axis=1)

    vmem = pl.BlockSpec(memory_space=pltpu.VMEM)
    hbm = pl.BlockSpec(memory_space=pl.ANY)
    dma = pltpu.SemaphoreType.DMA
    query, window = pl.pallas_call(
        functools.partial(project, n, nh, reach),
        out_shape=(
            jax.ShapeDtypeStruct((q_heads, rows, HEAD), BF16),
            jax.ShapeDtypeStruct((2 * kv_heads, (reach + 1) * rows, HEAD), BF16),
        ),
        in_specs=[hbm] * 4 + [vmem] * 4,
        out_specs=(vmem, vmem),
        scratch_shapes=[
            pltpu.VMEM((n, 4, slab, kv_cols), BF16),
            pltpu.VMEM((nh, sub, rows + GAIN_ROWS, slab), BF16),
            pltpu.VMEM((n, rows, slab), BF16),
            pltpu.VMEM((4, rows, kv_cols), F32),
            pltpu.VMEM((2 * kv_heads, (reach + 1) * rows, HEAD), BF16),
            dma((5,)), dma((nh - 1,)), dma((nh - 1,)),
            dma((2, half, 4)), dma((2, half, 4)), dma((2,)), dma((2,)),
        ],
        compiler_params=pltpu.CompilerParams(
            collective_id=0, has_side_effects=True, vmem_limit_bytes=60 * 2**20),
        name="project",
    )(extended, w_query, w_key, value_matrix, q_norm_gain, k_norm_gain, cosine, sine)

    ny = nh // 2
    block = rows // 2
    return pl.pallas_call(
        functools.partial(attend, nh, reach),
        out_shape=jax.ShapeDtypeStruct((rows, width), BF16),
        in_specs=[vmem] * 3,
        out_specs=vmem,
        scratch_shapes=[
            pltpu.VMEM((q_heads, block, HEAD), BF16),
            pltpu.VMEM((2, nh, block, width), BF16),
            pltpu.VMEM((2, ny, block, width), BF16),
            pltpu.VMEM((2, ny - 1, block, width), BF16),
            pltpu.VMEM((2, ny - 1, block, width), BF16),
            dma((2, ny)), dma((2, ny)), dma((2, ny - 1)), dma((2, ny - 1)),
        ],
        compiler_params=pltpu.CompilerParams(
            collective_id=1, has_side_effects=True, vmem_limit_bytes=56 * 2**20),
        name="attend",
    )(query, window, w_out)


def solution(mesh):
    in_specs = (
        P("tok", "hid"),
        P(None, "hid"),
        P("tok", "hid"),
        P("tok", "hid"),
        P("tok", "hid"),
        P(),
        P(),
        P("hid", None),
    )
    body = functools.partial(local, mesh.shape["tok"], mesh.shape["hid"])
    return jax.shard_map(
        body, mesh=mesh, in_specs=in_specs, out_specs=P("tok", "hid"), check_vma=False)
```

```python
import functools
import math

import jax
import jax.numpy as jnp
from jax import lax
from jax.experimental import pallas as pl
from jax.experimental.pallas import tpu as pltpu
from jax.sharding import PartitionSpec as P

HEAD = 128
WINDOW = 1024
SCALE = 168.0 ** (-0.5)
GAIN_ROWS = 16
MESH = pl.DeviceIdType.MESH
F32 = jnp.float32
BF16 = jnp.bfloat16


def tok_of(pos, n):
    pos = lax.rem(pos + 2 * n, n)
    return jnp.where(pos < n // 2, 2 * pos, 2 * (n - 1 - pos) + 1)


def project(n, nh, reach, x_ref, wq, wk, wv, qg, kg, cos_ref, sin_ref, q_out, win_out,
            w, xs, normed, acc, win, own_sem, x_send, x_recv, send_sem, recv_sem,
            halo_send, halo_recv):
    t = lax.axis_index("tok")
    h = lax.axis_index("hid")
    half = n // 2
    rows = q_out.shape[1]
    sub = x_ref.shape[0]
    part_heads = w.shape[3] // HEAD
    pos = jnp.where(lax.rem(t, 2) == 0, t // 2, n - 1 - t // 2)
    nxt = (tok_of(pos + 1, n), tok_of(pos - 1, n))

    barrier = pltpu.get_barrier_semaphore()
    near = list(nxt) + [lax.rem(t + d + n, n) for d in (1, -1, 2, -2)]
    for peer in near:
        pl.semaphore_signal(barrier, inc=1, device_id={"tok": peer}, device_id_type=MESH)
    for d in range(1, nh):
        pl.semaphore_signal(
            barrier, inc=1, device_id={"hid": lax.rem(h + d, nh)}, device_id_type=MESH)

    cols = w.shape[3]
    own = [
        pltpu.make_async_copy(src, w.at[t, p], own_sem.at[p])
        for p, src in enumerate((wk, wv, wq.at[:, pl.ds(0, cols)], wq.at[:, pl.ds(cols, cols)]))
    ]
    for copy in own:
        copy.start()
    own_x = pltpu.make_async_copy(x_ref, xs.at[h], own_sem.at[4])
    own_x.start()
    pl.semaphore_wait(barrier, len(near) + nh - 1)

    def hop(way, step, part):
        origin = tok_of(pos - step if way == 0 else pos + step, n)
        return pltpu.make_async_remote_copy(
            src_ref=w.at[origin, part], dst_ref=w.at[origin, part],
            send_sem=send_sem.at[way, step, part], recv_sem=recv_sem.at[way, step, part],
            device_id={"tok": nxt[way]}, device_id_type=MESH)

    def arrival(way, step, part):
        origin = tok_of(pos - step - 1 if way == 0 else pos + step + 1, n)
        return pltpu.make_async_remote_copy(
            src_ref=w.at[origin, part], dst_ref=w.at[origin, part],
            send_sem=send_sem.at[way, step, part], recv_sem=recv_sem.at[way, step, part],
            device_id={"tok": nxt[way]}, device_id_type=MESH)

    def carried(way, step, part):
        return step < half - 1 or part % 2 == way

    def launch(step, parts):
        for part in parts:
            for way in (0, 1):
                if carried(way, step, part):
                    if step == 0:
                        if way == 0:
                            own[part].wait()
                    else:
                        arrival(way, step - 1, part).wait_recv()
                    hop(way, step, part).start()

    def x_copy(d, slot):
        return pltpu.make_async_remote_copy(
            src_ref=x_ref, dst_ref=xs.at[slot], send_sem=x_send.at[d - 1],
            recv_sem=x_recv.at[d - 1],
            device_id={"hid": lax.rem(h + d, nh)}, device_id_type=MESH)

    kv, qq = (0, 1), (2, 3)
    launch(0, kv)
    for d in range(1, nh):
        x_copy(d, h).start()
    for step in range(1, half):
        launch(step, kv)
    launch(0, qq)

    own_x.wait()
    for d in range(1, nh):
        x_copy(d, lax.rem(h - d + nh, nh)).wait_recv()
    block = 128

    def norm_rows(i, _):
        at = pl.ds(pl.multiple_of(i * block, block), block)
        square = jnp.zeros((block, 1), F32)
        for b in range(nh):
            for j in range(sub):
                value = xs[b, j, at, :].astype(F32)
                square = square + jnp.sum(value * value, axis=1, keepdims=True)
        scale = lax.rsqrt(square / (nh * sub * x_ref.shape[2]) + 1e-06)
        for b in range(nh):
            for j in range(sub):
                value = xs[b, j, at, :].astype(F32)
                gain = xs[b, j, pl.ds(rows, GAIN_ROWS), :].astype(F32)[0:1]
                normed[b * sub + j, at, :] = (value * scale * gain).astype(BF16)
        return 0

    lax.fori_loop(0, rows // block, norm_rows, 0)

    def accumulate(part, slab):
        acc[part] += jnp.dot(normed[slab], w[slab, part], preferred_element_type=F32)

    def head_turned(part, j, gain):
        def place(i, _):
            at = pl.ds(pl.multiple_of(i * block, block), block)
            value = acc[part, at, j * HEAD:(j + 1) * HEAD]
            mean = jnp.sum(value * value, axis=1, keepdims=True) / HEAD
            value = value * lax.rsqrt(mean + 1e-06) * gain
            turned = value * cos_ref[at, :] + pltpu.roll(value, HEAD // 2, 1) * sin_ref[at, :]
            yield_at = turned.astype(BF16)
            if part == 0:
                at2 = pl.ds(pl.multiple_of(reach * rows + i * block, block), block)
                win[j, at2, :] = yield_at
            else:
                q_out[(part - 2) * part_heads + j, at, :] = yield_at
            return 0

        lax.fori_loop(0, rows // block, place, 0)

    for part in range(4):
        acc[part] = jnp.zeros(acc.shape[1:], F32)
    for way in (0, 1):
        arrival(way, half - 2, 1 - way).wait_recv()
    last = tok_of(pos + half, n)

    def kv_slab(i, _):
        slab = tok_of(pos - (half - 1) + i, n)
        accumulate(0, slab)
        accumulate(1, slab)
        return 0

    lax.fori_loop(0, n - 1, kv_slab, 0)
    for way in (0, 1):
        arrival(way, half - 1, way).wait_recv()
        accumulate(way, last)
    k_gain = kg[...].astype(F32)
    q_gain = qg[...].astype(F32)
    for j in range(part_heads):
        head_turned(0, j, k_gain)
        win[part_heads + j, pl.ds(reach * rows, rows), :] = (
            acc[1, :, j * HEAD:(j + 1) * HEAD].astype(BF16))

    even = lax.rem(t, 2) == 0
    mine = win.at[:, pl.ds(2 * rows, rows), :]
    far = win.at[:, pl.ds(0, rows), :]
    mid = win.at[:, pl.ds(rows, rows), :]

    def halo(k, src, dst, peer):
        return pltpu.make_async_remote_copy(
            src_ref=src, dst_ref=dst, send_sem=halo_send.at[k], recv_sem=halo_recv.at[k],
            device_id={"tok": lax.rem(peer + n, n)}, device_id_type=MESH)

    to_far = halo(0, mine, far, t + 2)
    to_mid = halo(1, mine, mid, t + 1)
    relay = halo(1, far, mid, t - 1)
    has_far = t >= 2
    has_mid = t >= 1
    gives_far = t + 2 < n
    relays = jnp.logical_and(jnp.logical_not(even), has_far)

    @pl.when(gives_far)
    def _():
        to_far.start()

    @pl.when(even)
    def _():
        to_mid.start()

    @pl.when(jnp.logical_not(has_far))
    def _():
        win[:, pl.ds(0, rows), :] = jnp.zeros((win.shape[0], rows, HEAD), BF16)

    @pl.when(jnp.logical_not(has_mid))
    def _():
        win[:, pl.ds(rows, rows), :] = jnp.zeros((win.shape[0], rows, HEAD), BF16)

    for step in range(1, half):
        if step == half - 1:
            @pl.when(has_far)
            def _():
                to_far.wait_recv()

            @pl.when(relays)
            def _():
                relay.start()
        launch(step, qq)

    for way in (0, 1):
        arrival(way, half - 2, 3 - way).wait_recv()

    def q_slab(i, _):
        slab = tok_of(pos - (half - 1) + i, n)
        accumulate(2, slab)
        accumulate(3, slab)
        return 0

    lax.fori_loop(0, n - 1, q_slab, 0)
    for way in (0, 1):
        arrival(way, half - 1, 2 + way).wait_recv()
        accumulate(2 + way, last)
        for j in range(part_heads):
            head_turned(2 + way, j, q_gain)

    @pl.when(has_mid)
    def _():
        to_mid.wait_recv()

    win_out[...] = win[...]

    @pl.when(gives_far)
    def _():
        to_far.wait_send()

    @pl.when(even)
    def _():
        to_mid.wait_send()

    @pl.when(relays)
    def _():
        relay.wait_send()

    for d in range(1, nh):
        x_copy(d, h).wait_send()
    for parts in (kv, qq):
        for step in range(half):
            for part in parts:
                for way in (0, 1):
                    if carried(way, step, part):
                        hop(way, step, part).wait_send()


def attend(nh, reach, q_ref, win_ref, wo_hbm, out_ref, wo_ref, heads, part, sib, pair, got,
           wo_sem, sib_send, sib_recv, y_send, y_recv):
    t = lax.axis_index("tok")
    h = lax.axis_index("hid")
    ny = nh // 2
    y, core = h // 2, lax.rem(h, 2)
    q_heads, rows = q_ref.shape[0], q_ref.shape[1]
    kv_heads = win_ref.shape[0] // 2
    group = q_heads // kv_heads
    width = out_ref.shape[1]
    block = rows // 2
    extent = block + WINDOW

    wo_copy = pltpu.make_async_copy(wo_hbm, wo_ref, wo_sem)
    wo_copy.start()
    barrier = pltpu.get_barrier_semaphore()
    for d in range(1, nh):
        pl.semaphore_signal(
            barrier, inc=1, device_id={"hid": lax.rem(h + d, nh)}, device_id_type=MESH)

    def attention(r):
        ahead = reach * rows + r * block - WINDOW
        row = lax.broadcasted_iota(jnp.int32, (block, extent), 0)
        col = lax.broadcasted_iota(jnp.int32, (block, extent), 1)
        first = reach * rows - t * rows - ahead
        allowed = (col <= row + WINDOW) & (col > row) & (col >= first)

        def head(i, _):
            k = win_ref[i, pl.ds(ahead, extent), :]
            v = win_ref[kv_heads + i, pl.ds(ahead, extent), :]
            for g in range(group):
                q = q_ref[i * group + g, pl.ds(r * block, block), :]
                s = lax.dot_general(
                    q, k, (((1,), (1,)), ((), ())), preferred_element_type=F32)
                s = jnp.where(allowed, s, -1e30)
                top = jnp.max(s, axis=1, keepdims=True)
                weights = jnp.exp2((s - top) * (SCALE * math.log2(math.e)))
                total = jnp.sum(weights, axis=1, keepdims=True)
                mixed = jnp.dot(weights.astype(BF16), v, preferred_element_type=F32) / total
                heads[i * group + g] = mixed.astype(BF16)
            return 0

        lax.fori_loop(0, kv_heads, head, 0)

    def to_sibling(r, k):
        y2 = lax.rem(y + k, ny)
        return pltpu.make_async_remote_copy(
            src_ref=part.at[r, y2 * 2 + 1 - core], dst_ref=sib.at[r, k],
            send_sem=sib_send.at[r, k], recv_sem=sib_recv.at[r, k],
            device_id={"hid": y * 2 + 1 - core}, device_id_type=MESH)

    def across(r, k):
        y2 = lax.rem(y + k, ny)
        return pltpu.make_async_remote_copy(
            src_ref=pair.at[r, k - 1], dst_ref=got.at[r, k - 1],
            send_sem=y_send.at[r, k - 1], recv_sem=y_recv.at[r, k - 1],
            device_id={"hid": y2 * 2 + core}, device_id_type=MESH)

    def project_block(r, b):
        mixed = jnp.concatenate([heads[i] for i in range(q_heads)], axis=1)
        start, end = b * width, (b + 1) * width
        a, e = start // 128 * 128, -(-end // 128) * 128
        value = jnp.dot(mixed, wo_ref[:, a:e], preferred_element_type=F32)
        if start > a:
            value = pltpu.roll(value, (e - a) - (start - a), 1)
        part[r, b] = value[:, :width].astype(BF16)

    def out_project(r, k):
        for y2 in range(ny):
            @pl.when(lax.rem(y + k, ny) == y2)
            def _():
                project_block(r, 2 * y2)
                project_block(r, 2 * y2 + 1)

    order = list(range(1, ny)) + [0]

    def pass_on(r):
        for k in range(1, ny):
            to_sibling(r, k).wait_recv()
            y2 = lax.rem(y + k, ny)
            pair[r, k - 1] = (
                part[r, y2 * 2 + core].astype(F32) + sib[r, k].astype(F32)).astype(BF16)
            across(r, k).start()

    def finish(r):
        to_sibling(r, 0).wait_recv()
        value = part[r, h].astype(F32) + sib[r, 0].astype(F32)
        for k in range(1, ny):
            across(r, k).wait_recv()
            value = value + got[r, k - 1].astype(F32)
        out_ref[pl.ds(r * block, block), :] = value.astype(BF16)

    for r in range(2):
        attention(r)
        if r == 0:
            pl.semaphore_wait(barrier, nh - 1)
            wo_copy.wait()
        for k in order:
            if k == 0:
                pass_on(r)
            out_project(r, k)
            to_sibling(r, k).start()
    for r in range(2):
        finish(r)
    for r in range(2):
        for k in order:
            to_sibling(r, k).wait_send()
        for k in range(1, ny):
            across(r, k).wait_send()


def local(n, nh, tokens, norm_gain, w_query, w_key, value_matrix, q_norm_gain, k_norm_gain, w_out):
    rows, feat = tokens.shape
    slab, kv_cols = w_key.shape
    sub = feat // slab
    q_heads, kv_heads = w_query.shape[1] // HEAD, kv_cols // HEAD
    reach = (WINDOW - 1 + rows - 1) // rows
    width = w_out.shape[1] // nh
    half = n // 2
    extended = jnp.concatenate(
        [tokens, jnp.broadcast_to(norm_gain, (GAIN_ROWS, feat))], axis=0)
    extended = jnp.transpose(extended.reshape(rows + GAIN_ROWS, sub, slab), (1, 0, 2))
    inverse = jnp.exp(
        -math.log(10000.0) * jnp.arange(HEAD // 2, dtype=F32) * 2.0 / HEAD)
    positions = lax.axis_index("tok") * rows + jnp.arange(rows, dtype=jnp.int32)
    angles = positions.astype(F32)[:, None] * inverse[None, :]
    cosine, sine = jnp.cos(angles), jnp.sin(angles)
    cosine = jnp.concatenate([cosine, cosine], axis=1)
    sine = jnp.concatenate([-sine, sine], axis=1)

    vmem = pl.BlockSpec(memory_space=pltpu.VMEM)
    hbm = pl.BlockSpec(memory_space=pl.ANY)
    dma = pltpu.SemaphoreType.DMA
    query, window = pl.pallas_call(
        functools.partial(project, n, nh, reach),
        out_shape=(
            jax.ShapeDtypeStruct((q_heads, rows, HEAD), BF16),
            jax.ShapeDtypeStruct((2 * kv_heads, (reach + 1) * rows, HEAD), BF16),
        ),
        in_specs=[hbm] * 4 + [vmem] * 4,
        out_specs=(vmem, vmem),
        scratch_shapes=[
            pltpu.VMEM((n, 4, slab, kv_cols), BF16),
            pltpu.VMEM((nh, sub, rows + GAIN_ROWS, slab), BF16),
            pltpu.VMEM((n, rows, slab), BF16),
            pltpu.VMEM((4, rows, kv_cols), F32),
            pltpu.VMEM((2 * kv_heads, (reach + 1) * rows, HEAD), BF16),
            dma((5,)), dma((nh - 1,)), dma((nh - 1,)),
            dma((2, half, 4)), dma((2, half, 4)), dma((2,)), dma((2,)),
        ],
        compiler_params=pltpu.CompilerParams(
            collective_id=0, has_side_effects=True, vmem_limit_bytes=60 * 2**20),
        name="project",
    )(extended, w_query, w_key, value_matrix, q_norm_gain, k_norm_gain, cosine, sine)

    ny = nh // 2
    block = rows // 2
    return pl.pallas_call(
        functools.partial(attend, nh, reach),
        out_shape=jax.ShapeDtypeStruct((rows, width), BF16),
        in_specs=[vmem, vmem, hbm],
        out_specs=vmem,
        scratch_shapes=[
            pltpu.VMEM(w_out.shape, BF16),
            pltpu.VMEM((q_heads, block, HEAD), BF16),
            pltpu.VMEM((2, nh, block, width), BF16),
            pltpu.VMEM((2, ny, block, width), BF16),
            pltpu.VMEM((2, ny - 1, block, width), BF16),
            pltpu.VMEM((2, ny - 1, block, width), BF16),
            dma(()), dma((2, ny)), dma((2, ny)), dma((2, ny - 1)), dma((2, ny - 1)),
        ],
        compiler_params=pltpu.CompilerParams(
            collective_id=1, has_side_effects=True, vmem_limit_bytes=56 * 2**20),
        name="attend",
    )(query, window, w_out)


def solution(mesh):
    in_specs = (
        P("tok", "hid"),
        P(None, "hid"),
        P("tok", "hid"),
        P("tok", "hid"),
        P("tok", "hid"),
        P(),
        P(),
        P("hid", None),
    )
    body = functools.partial(local, mesh.shape["tok"], mesh.shape["hid"])
    return jax.shard_map(
        body, mesh=mesh, in_specs=in_specs, out_specs=P("tok", "hid"), check_vma=False)
```

```python
import functools
import math

import jax
import jax.numpy as jnp
from jax import lax
from jax.experimental import pallas as pl
from jax.experimental.pallas import tpu as pltpu
from jax.sharding import PartitionSpec as P

HEAD = 128
WINDOW = 1024
SCALE = 168.0 ** (-0.5)
GAIN_ROWS = 16
BLOCKS = 4
MESH = pl.DeviceIdType.MESH
F32 = jnp.float32
BF16 = jnp.bfloat16


def tok_of(pos, n):
    pos = lax.rem(pos + 2 * n, n)
    return jnp.where(pos < n // 2, 2 * pos, 2 * (n - 1 - pos) + 1)


def project(n, nh, reach, x_ref, wq, wk, wv, qg, kg, cos_ref, sin_ref, q_out, win_out,
            w, xs, normed, acc, win, own_sem, x_send, x_recv, send_sem, recv_sem,
            halo_send, halo_recv):
    t = lax.axis_index("tok")
    h = lax.axis_index("hid")
    half = n // 2
    rows = q_out.shape[1]
    sub = x_ref.shape[0]
    part_heads = w.shape[3] // HEAD
    pos = jnp.where(lax.rem(t, 2) == 0, t // 2, n - 1 - t // 2)
    nxt = (tok_of(pos + 1, n), tok_of(pos - 1, n))

    barrier = pltpu.get_barrier_semaphore()
    near = list(nxt) + [lax.rem(t + d + n, n) for d in (1, -1, 2, -2)]
    for peer in near:
        pl.semaphore_signal(barrier, inc=1, device_id={"tok": peer}, device_id_type=MESH)
    for d in range(1, nh):
        pl.semaphore_signal(
            barrier, inc=1, device_id={"hid": lax.rem(h + d, nh)}, device_id_type=MESH)

    cols = w.shape[3]
    own = [
        pltpu.make_async_copy(src, w.at[t, p], own_sem.at[p])
        for p, src in enumerate((wk, wv, wq.at[:, pl.ds(0, cols)], wq.at[:, pl.ds(cols, cols)]))
    ]
    for copy in own:
        copy.start()
    own_x = pltpu.make_async_copy(x_ref, xs.at[h], own_sem.at[4])
    own_x.start()
    pl.semaphore_wait(barrier, len(near) + nh - 1)

    def hop(way, step, part):
        origin = tok_of(pos - step if way == 0 else pos + step, n)
        return pltpu.make_async_remote_copy(
            src_ref=w.at[origin, part], dst_ref=w.at[origin, part],
            send_sem=send_sem.at[way, step, part], recv_sem=recv_sem.at[way, step, part],
            device_id={"tok": nxt[way]}, device_id_type=MESH)

    def arrival(way, step, part):
        origin = tok_of(pos - step - 1 if way == 0 else pos + step + 1, n)
        return pltpu.make_async_remote_copy(
            src_ref=w.at[origin, part], dst_ref=w.at[origin, part],
            send_sem=send_sem.at[way, step, part], recv_sem=recv_sem.at[way, step, part],
            device_id={"tok": nxt[way]}, device_id_type=MESH)

    def carried(way, step, part):
        return step < half - 1 or part % 2 == way

    def launch(step, parts):
        for part in parts:
            for way in (0, 1):
                if carried(way, step, part):
                    if step == 0:
                        if way == 0:
                            own[part].wait()
                    else:
                        arrival(way, step - 1, part).wait_recv()
                    hop(way, step, part).start()

    def x_copy(d, slot):
        return pltpu.make_async_remote_copy(
            src_ref=x_ref, dst_ref=xs.at[slot], send_sem=x_send.at[d - 1],
            recv_sem=x_recv.at[d - 1],
            device_id={"hid": lax.rem(h + d, nh)}, device_id_type=MESH)

    kv, qq = (0, 1), (2, 3)
    launch(0, kv)
    for d in range(1, nh):
        x_copy(d, h).start()
    for step in range(1, half):
        launch(step, kv)
    launch(0, qq)

    own_x.wait()
    for d in range(1, nh):
        x_copy(d, lax.rem(h - d + nh, nh)).wait_recv()
    block = 128

    def norm_rows(i, _):
        at = pl.ds(pl.multiple_of(i * block, block), block)
        square = jnp.zeros((block, 1), F32)
        for b in range(nh):
            for j in range(sub):
                value = xs[b, j, at, :].astype(F32)
                square = square + jnp.sum(value * value, axis=1, keepdims=True)
        scale = lax.rsqrt(square / (nh * sub * x_ref.shape[2]) + 1e-06)
        for b in range(nh):
            for j in range(sub):
                value = xs[b, j, at, :].astype(F32)
                gain = xs[b, j, pl.ds(rows, GAIN_ROWS), :].astype(F32)[0:1]
                normed[b * sub + j, at, :] = (value * scale * gain).astype(BF16)
        return 0

    lax.fori_loop(0, rows // block, norm_rows, 0)

    def accumulate(part, slab):
        acc[part] += jnp.dot(normed[slab], w[slab, part], preferred_element_type=F32)

    def head_turned(part, j, gain):
        def place(i, _):
            at = pl.ds(pl.multiple_of(i * block, block), block)
            value = acc[part, at, j * HEAD:(j + 1) * HEAD]
            mean = jnp.sum(value * value, axis=1, keepdims=True) / HEAD
            value = value * lax.rsqrt(mean + 1e-06) * gain
            turned = value * cos_ref[at, :] + pltpu.roll(value, HEAD // 2, 1) * sin_ref[at, :]
            yield_at = turned.astype(BF16)
            if part == 0:
                at2 = pl.ds(pl.multiple_of(reach * rows + i * block, block), block)
                win[j, at2, :] = yield_at
            else:
                q_out[(part - 2) * part_heads + j, at, :] = yield_at
            return 0

        lax.fori_loop(0, rows // block, place, 0)

    for part in range(4):
        acc[part] = jnp.zeros(acc.shape[1:], F32)
    for way in (0, 1):
        arrival(way, half - 2, 1 - way).wait_recv()
    last = tok_of(pos + half, n)

    def kv_slab(i, _):
        slab = tok_of(pos - (half - 1) + i, n)
        accumulate(0, slab)
        accumulate(1, slab)
        return 0

    lax.fori_loop(0, n - 1, kv_slab, 0)
    for way in (0, 1):
        arrival(way, half - 1, way).wait_recv()
        accumulate(way, last)
    k_gain = kg[...].astype(F32)
    q_gain = qg[...].astype(F32)
    for j in range(part_heads):
        head_turned(0, j, k_gain)
        win[part_heads + j, pl.ds(reach * rows, rows), :] = (
            acc[1, :, j * HEAD:(j + 1) * HEAD].astype(BF16))

    even = lax.rem(t, 2) == 0
    mine = win.at[:, pl.ds(2 * rows, rows), :]
    far = win.at[:, pl.ds(0, rows), :]
    mid = win.at[:, pl.ds(rows, rows), :]

    def halo(k, src, dst, peer):
        return pltpu.make_async_remote_copy(
            src_ref=src, dst_ref=dst, send_sem=halo_send.at[k], recv_sem=halo_recv.at[k],
            device_id={"tok": lax.rem(peer + n, n)}, device_id_type=MESH)

    to_far = halo(0, mine, far, t + 2)
    to_mid = halo(1, mine, mid, t + 1)
    relay = halo(1, far, mid, t - 1)
    has_far = t >= 2
    has_mid = t >= 1
    gives_far = t + 2 < n
    relays = jnp.logical_and(jnp.logical_not(even), has_far)

    @pl.when(gives_far)
    def _():
        to_far.start()

    @pl.when(even)
    def _():
        to_mid.start()

    @pl.when(jnp.logical_not(has_far))
    def _():
        win[:, pl.ds(0, rows), :] = jnp.zeros((win.shape[0], rows, HEAD), BF16)

    @pl.when(jnp.logical_not(has_mid))
    def _():
        win[:, pl.ds(rows, rows), :] = jnp.zeros((win.shape[0], rows, HEAD), BF16)

    for step in range(1, half):
        if step == half - 1:
            @pl.when(has_far)
            def _():
                to_far.wait_recv()

            @pl.when(relays)
            def _():
                relay.start()
        launch(step, qq)

    for way in (0, 1):
        arrival(way, half - 2, 3 - way).wait_recv()

    def q_slab(i, _):
        slab = tok_of(pos - (half - 1) + i, n)
        accumulate(2, slab)
        accumulate(3, slab)
        return 0

    lax.fori_loop(0, n - 1, q_slab, 0)
    for way in (0, 1):
        arrival(way, half - 1, 2 + way).wait_recv()
        accumulate(2 + way, last)
        for j in range(part_heads):
            head_turned(2 + way, j, q_gain)

    @pl.when(has_mid)
    def _():
        to_mid.wait_recv()

    win_out[...] = win[...]

    @pl.when(gives_far)
    def _():
        to_far.wait_send()

    @pl.when(even)
    def _():
        to_mid.wait_send()

    @pl.when(relays)
    def _():
        relay.wait_send()

    for d in range(1, nh):
        x_copy(d, h).wait_send()
    for parts in (kv, qq):
        for step in range(half):
            for part in parts:
                for way in (0, 1):
                    if carried(way, step, part):
                        hop(way, step, part).wait_send()


def attend(nh, reach, q_ref, win_ref, wo_hbm, out_ref, wo_ref, heads, part, sib, pair, got,
           wo_sem, sib_send, sib_recv, y_send, y_recv):
    t = lax.axis_index("tok")
    h = lax.axis_index("hid")
    ny = nh // 2
    y, core = h // 2, lax.rem(h, 2)
    q_heads, rows = q_ref.shape[0], q_ref.shape[1]
    kv_heads = win_ref.shape[0] // 2
    group = q_heads // kv_heads
    width = out_ref.shape[1]
    block = rows // BLOCKS
    extent = block + WINDOW

    wo_copy = pltpu.make_async_copy(wo_hbm, wo_ref, wo_sem)
    wo_copy.start()
    barrier = pltpu.get_barrier_semaphore()
    for d in range(1, nh):
        pl.semaphore_signal(
            barrier, inc=1, device_id={"hid": lax.rem(h + d, nh)}, device_id_type=MESH)

    def attention(r):
        ahead = reach * rows + r * block - WINDOW
        row = lax.broadcasted_iota(jnp.int32, (block, extent), 0)
        col = lax.broadcasted_iota(jnp.int32, (block, extent), 1)
        first = reach * rows - t * rows - ahead
        allowed = (col <= row + WINDOW) & (col > row) & (col >= first)

        def head(i, _):
            k = win_ref[i, pl.ds(ahead, extent), :]
            v = win_ref[kv_heads + i, pl.ds(ahead, extent), :]
            for g in range(group):
                q = q_ref[i * group + g, pl.ds(r * block, block), :]
                s = lax.dot_general(
                    q, k, (((1,), (1,)), ((), ())), preferred_element_type=F32)
                s = jnp.where(allowed, s, -1e30)
                top = jnp.max(s, axis=1, keepdims=True)
                weights = jnp.exp2((s - top) * (SCALE * math.log2(math.e)))
                total = jnp.sum(weights, axis=1, keepdims=True)
                mixed = jnp.dot(weights.astype(BF16), v, preferred_element_type=F32) / total
                heads[i * group + g] = mixed.astype(BF16)
            return 0

        lax.fori_loop(0, kv_heads, head, 0)

    def to_sibling(r, k):
        y2 = lax.rem(y + k, ny)
        return pltpu.make_async_remote_copy(
            src_ref=part.at[r, y2 * 2 + 1 - core], dst_ref=sib.at[r, k],
            send_sem=sib_send.at[r, k], recv_sem=sib_recv.at[r, k],
            device_id={"hid": y * 2 + 1 - core}, device_id_type=MESH)

    def across(r, k):
        y2 = lax.rem(y + k, ny)
        return pltpu.make_async_remote_copy(
            src_ref=pair.at[r, k - 1], dst_ref=got.at[r, k - 1],
            send_sem=y_send.at[r, k - 1], recv_sem=y_recv.at[r, k - 1],
            device_id={"hid": y2 * 2 + core}, device_id_type=MESH)

    def project_block(r, b):
        mixed = jnp.concatenate([heads[i] for i in range(q_heads)], axis=1)
        start, end = b * width, (b + 1) * width
        a, e = start // 128 * 128, -(-end // 128) * 128
        value = jnp.dot(mixed, wo_ref[:, a:e], preferred_element_type=F32)
        if start > a:
            value = pltpu.roll(value, (e - a) - (start - a), 1)
        part[r, b] = value[:, :width].astype(BF16)

    def out_project(r, k):
        for y2 in range(ny):
            @pl.when(lax.rem(y + k, ny) == y2)
            def _():
                project_block(r, 2 * y2)
                project_block(r, 2 * y2 + 1)

    order = list(range(1, ny)) + [0]

    def pass_on(r):
        for k in range(1, ny):
            to_sibling(r, k).wait_recv()
            y2 = lax.rem(y + k, ny)
            pair[r, k - 1] = (
                part[r, y2 * 2 + core].astype(F32) + sib[r, k].astype(F32)).astype(BF16)
            across(r, k).start()

    def finish(r):
        to_sibling(r, 0).wait_recv()
        value = part[r, h].astype(F32) + sib[r, 0].astype(F32)
        for k in range(1, ny):
            across(r, k).wait_recv()
            value = value + got[r, k - 1].astype(F32)
        out_ref[pl.ds(r * block, block), :] = value.astype(BF16)

    for r in range(BLOCKS):
        attention(r)
        if r == 0:
            pl.semaphore_wait(barrier, nh - 1)
            wo_copy.wait()
        for k in order:
            if k == 0:
                pass_on(r)
            out_project(r, k)
            to_sibling(r, k).start()
    for r in range(BLOCKS):
        finish(r)
    for r in range(BLOCKS):
        for k in order:
            to_sibling(r, k).wait_send()
        for k in range(1, ny):
            across(r, k).wait_send()


def local(n, nh, tokens, norm_gain, w_query, w_key, value_matrix, q_norm_gain, k_norm_gain, w_out):
    rows, feat = tokens.shape
    slab, kv_cols = w_key.shape
    sub = feat // slab
    q_heads, kv_heads = w_query.shape[1] // HEAD, kv_cols // HEAD
    reach = (WINDOW - 1 + rows - 1) // rows
    width = w_out.shape[1] // nh
    half = n // 2
    extended = jnp.concatenate(
        [tokens, jnp.broadcast_to(norm_gain, (GAIN_ROWS, feat))], axis=0)
    extended = jnp.transpose(extended.reshape(rows + GAIN_ROWS, sub, slab), (1, 0, 2))
    inverse = jnp.exp(
        -math.log(10000.0) * jnp.arange(HEAD // 2, dtype=F32) * 2.0 / HEAD)
    positions = lax.axis_index("tok") * rows + jnp.arange(rows, dtype=jnp.int32)
    angles = positions.astype(F32)[:, None] * inverse[None, :]
    cosine, sine = jnp.cos(angles), jnp.sin(angles)
    cosine = jnp.concatenate([cosine, cosine], axis=1)
    sine = jnp.concatenate([-sine, sine], axis=1)

    vmem = pl.BlockSpec(memory_space=pltpu.VMEM)
    hbm = pl.BlockSpec(memory_space=pl.ANY)
    dma = pltpu.SemaphoreType.DMA
    query, window = pl.pallas_call(
        functools.partial(project, n, nh, reach),
        out_shape=(
            jax.ShapeDtypeStruct((q_heads, rows, HEAD), BF16),
            jax.ShapeDtypeStruct((2 * kv_heads, (reach + 1) * rows, HEAD), BF16),
        ),
        in_specs=[hbm] * 4 + [vmem] * 4,
        out_specs=(vmem, vmem),
        scratch_shapes=[
            pltpu.VMEM((n, 4, slab, kv_cols), BF16),
            pltpu.VMEM((nh, sub, rows + GAIN_ROWS, slab), BF16),
            pltpu.VMEM((n, rows, slab), BF16),
            pltpu.VMEM((4, rows, kv_cols), F32),
            pltpu.VMEM((2 * kv_heads, (reach + 1) * rows, HEAD), BF16),
            dma((5,)), dma((nh - 1,)), dma((nh - 1,)),
            dma((2, half, 4)), dma((2, half, 4)), dma((2,)), dma((2,)),
        ],
        compiler_params=pltpu.CompilerParams(
            collective_id=0, has_side_effects=True, vmem_limit_bytes=60 * 2**20),
        name="project",
    )(extended, w_query, w_key, value_matrix, q_norm_gain, k_norm_gain, cosine, sine)

    ny = nh // 2
    block = rows // BLOCKS
    return pl.pallas_call(
        functools.partial(attend, nh, reach),
        out_shape=jax.ShapeDtypeStruct((rows, width), BF16),
        in_specs=[vmem, vmem, hbm],
        out_specs=vmem,
        scratch_shapes=[
            pltpu.VMEM(w_out.shape, BF16),
            pltpu.VMEM((q_heads, block, HEAD), BF16),
            pltpu.VMEM((BLOCKS, nh, block, width), BF16),
            pltpu.VMEM((BLOCKS, ny, block, width), BF16),
            pltpu.VMEM((BLOCKS, ny - 1, block, width), BF16),
            pltpu.VMEM((BLOCKS, ny - 1, block, width), BF16),
            dma(()), dma((BLOCKS, ny)), dma((BLOCKS, ny)), dma((BLOCKS, ny - 1)), dma((BLOCKS, ny - 1)),
        ],
        compiler_params=pltpu.CompilerParams(
            collective_id=1, has_side_effects=True, vmem_limit_bytes=56 * 2**20),
        name="attend",
    )(query, window, w_out)


def solution(mesh):
    in_specs = (
        P("tok", "hid"),
        P(None, "hid"),
        P("tok", "hid"),
        P("tok", "hid"),
        P("tok", "hid"),
        P(),
        P(),
        P("hid", None),
    )
    body = functools.partial(local, mesh.shape["tok"], mesh.shape["hid"])
    return jax.shard_map(
        body, mesh=mesh, in_specs=in_specs, out_specs=P("tok", "hid"), check_vma=False)
```
